256 devices in a mesh: cuts: 16 (over x, y), det: 2 (over core), bank: 8 (over z).
Axes of the slice: x: 4, y: 4, z: 8, core: 2. Of those that a mesh axis runs over, the one named last changes fastest.
Arguments:
- strain: bfloat16 [16, 2, 6144], P('cuts', 'det'), may hold values from -6 to 6
- filters: bfloat16 [128, 256, 2048], P(('bank', 'cuts')), parts along dimension 0, may hold values from -0.125 to 0.125
- recon_weights: bfloat16 [128, 512, 256], P(('bank', 'cuts')), parts along dimension 0, may hold values from -0.09375 to 0.09375
- row_spans: int32 [4096], P('bank'), parts along dimension 0, may hold values from 1 to 16
- slice_rates: int32 [16], replicated, may hold values from 1 to 8, as said below
- delays: int32 [64, 2], replicated, may hold values from 0 to 47
- antenna: float32 [64, 2], replicated, may hold values from 0.2 to 1
Outputs:
- peak_amplitude: float32 [4096, 4096], P(('bank', 'cuts', 'det')), parts along dimension 0
The draws below stay inside these ranges and needn't reach their ends.
There are 8 independent parts, one for each index of `bank`. The reference program is written for one: setup_inputs(seed, part) draws one part's arguments, and reference() takes and returns one part's arrays. A program takes and returns all parts, laid end to end along the dimension named above; an argument that names none is the same for every part. Nothing has to cross between parts.
Inputs may be any that keep to these rules, and one draw needn't show every extreme that they name: `slice_rates`: every entry is a power of two; entries never fall along the slices; the first is 1 and the last is 8.
All inputs are finite; a program needn't handle non-finite values.
Results may differ from the reference program's by a relative error of at most 0.0014.
Values sent between devices are 32-bit elements; how exact they have to be, the bound alone decides.
No kernel may reach another device: no remote copies, remote signals or barrier semaphores. Data moves between devices by JAX's collectives and lax.ppermute only.
A program may use at most 64 MiB of HBM per device.

```python
import jax
import jax.numpy as jnp
from jax import lax

WIN = 4096
TAPS = 2048
BASES = 256
FMAX = 8
DIRS = 64
MAXD = 48
SLICES = 16
DETS = 2
ROWS = 512
N_CUTS = 16


def draw_slice_rates(key, part):
    top_level = FMAX.bit_length() - 1
    levels = jnp.sort(jax.random.randint(key, (SLICES,), 0, top_level + 1))
    levels = levels.at[0].set(0).at[SLICES - 1].set(top_level)
    return jnp.left_shift(jnp.ones((SLICES,), jnp.int32), levels).astype(jnp.int32)


def place_ends(values, stream_key, least, high):
    extent = values.shape
    index_at = [jax.random.randint(jax.random.fold_in(stream_key, axis), (), 0, extent[axis]) for axis in range(len(extent))]
    values = values.at[tuple(index_at)].set(least)
    longest = extent.index(max(extent))
    index_at[longest] = (index_at[longest] + 1) % extent[longest]
    return values.at[tuple(index_at)].set(high)


def level_of(key, shape, shards, smallest, largest):
    def one(dim, parts):
        steps = jax.random.uniform(jax.random.fold_in(jax.random.fold_in(key, 6), dim), (parts,), jnp.float32, smallest / len(shards), largest / len(shards))
        return jnp.repeat(jnp.exp(steps), shape[dim] // parts).reshape((-1,) + (1,) * (len(shape) - dim - 1))

    gain = one(*shards[0])
    for cut in shards[1:]:
        gain = gain * one(*cut)
    return gain


def noise(rng, dims, deviation, most, cuts=(), kind=jnp.bfloat16):
    level = level_of(rng, dims, cuts, -0.22, 0.18) if cuts else 1.0
    drawn = jax.random.normal(rng, dims, jnp.float32) * deviation * level
    return jnp.minimum(jnp.maximum(drawn, -most), most).astype(kind)


def setup_inputs(seed: int = 0, part: int = 0) -> dict:
    key_of = jax.random.split(jax.random.key(seed), 8)
    own_keys = jax.random.split(jax.random.fold_in(key_of[7], part), 8)
    return {
        "strain": noise(key_of[0], (SLICES, DETS, TAPS + WIN), 1.0, 6.0, ((0, 16), (1, 2))),
        "filters": noise(own_keys[1], (SLICES, BASES, TAPS), TAPS ** -0.5, 0.125, ((0, 16),)),
        "recon_weights": noise(own_keys[2], (SLICES, ROWS, BASES), (BASES * N_CUTS) ** -0.5, 0.09375, ((0, 16),)),
        "row_spans": place_ends(jax.random.randint(own_keys[3], (ROWS,), 1, SLICES + 1), jax.random.fold_in(own_keys[3], 1), 1, SLICES).astype(jnp.int32),
        "slice_rates": draw_slice_rates(jax.random.fold_in(key_of[7], 71), part),
        "delays": place_ends(jax.random.randint(key_of[5], (DIRS, DETS), 0, MAXD), jax.random.fold_in(key_of[5], 1), 0, MAXD - 1).astype(jnp.int32),
        "antenna": jnp.clip(jax.random.uniform(key_of[6], (DIRS, DETS), jnp.float32, 0.2, 1.0), 0.2, 1.0),
    }


def filter_reference(samples, bank):
    size = 2 * TAPS + WIN
    spectrum = jnp.fft.rfft(samples.astype(jnp.float32), n=size)
    kernel = jnp.fft.rfft(bank.astype(jnp.float32), n=size, axis=1)
    convolved = jnp.fft.irfft(kernel * spectrum[None, :], n=size, axis=1)
    return convolved[:, TAPS:TAPS + WIN].astype(jnp.bfloat16)


def coherent(series, delays, antenna):
    detectors, height, window = series.shape
    padded = jnp.concatenate([series, jnp.zeros((detectors, height, MAXD), series.dtype)], axis=2)

    def direction(number, highest):
        summed = jnp.zeros((height, window), jnp.float32)
        for detector in range(detectors):
            shifted = lax.dynamic_slice_in_dim(padded[detector], delays[number, detector], window, 1)
            summed = summed + antenna[number, detector] * shifted
        return jnp.maximum(highest, jnp.abs(summed))

    return lax.fori_loop(0, delays.shape[0], direction, jnp.zeros((height, window), jnp.float32))


def reference(strain, filters, recon_weights, row_spans, slice_rates, delays, antenna):
    moments = jnp.arange(WIN, dtype=jnp.int32)

    def one_slice(total, inputs):
        samples, bank, weights, factor, number = inputs
        filtered = jax.vmap(filter_reference, in_axes=(0, None))(samples, bank)
        rebuilt = jnp.einsum("rb,kbw->krw", weights.astype(jnp.float32), filtered.astype(jnp.float32))
        keeping = (number < row_spans).astype(jnp.float32)
        terms = rebuilt * keeping[None, :, None]
        widened = jnp.take(terms, moments // factor, axis=2)
        return total + widened, None

    numbers = jnp.arange(SLICES, dtype=jnp.int32)
    combined, unused = lax.scan(one_slice, jnp.zeros((DETS, ROWS, WIN), jnp.float32), (strain, filters, recon_weights, slice_rates, numbers))
    return coherent(combined, delays, antenna)
```

```python
import jax
import jax.numpy as jnp
from jax import lax
from jax.experimental import pallas as pl
from jax.experimental.pallas import tpu as pltpu
from jax.sharding import PartitionSpec as P

PHASES = 16
LANES = 128
BLOCK = 256


def interleave(tiles, lane):
    def swap(tiles, bit, lane_bit):
        step = 1 << lane_bit
        upper = (lane & step) != 0
        result = list(tiles)
        for v in range(PHASES):
            if v & (1 << bit):
                continue
            low, high = tiles[v], tiles[v | (1 << bit)]
            result[v] = jnp.where(upper, pltpu.roll(high, step, 1), low)
            result[v | (1 << bit)] = jnp.where(upper, high, pltpu.roll(low, LANES - step, 1))
        return result

    for bit in range(4):
        tiles = swap(tiles, bit, bit)
    for bit in range(3):
        tiles = swap(tiles, bit, bit + 4)
    return tiles


def kernel(rates, delays, antenna, g_ref, v_ref, out_ref, toeplitz, hankel, full, half, small, spread):
    step = pl.program_id(0)
    last = pl.num_programs(0) - 1
    rows, taps = g_ref.shape[1], g_ref.shape[2]
    detectors, blocks = v_ref.shape[1], v_ref.shape[2]
    depth = taps // BLOCK + 1
    directions = delays.shape[0]

    @pl.when(step == 0)
    def _():
        full[...] = jnp.zeros_like(full)
        half[...] = jnp.zeros_like(half)
        small[...] = jnp.zeros_like(small)

    lane8 = lax.broadcasted_iota(jnp.int32, (8, LANES), 1)
    turn = 16 + 16 * lax.broadcasted_iota(jnp.int32, (8, LANES), 0)
    first = lane8 < turn

    def turned(k, a, tile):
        piece = v_ref[0, k, a : a + 1, tile * LANES : (tile + 1) * LANES]
        return pltpu.roll(jnp.broadcast_to(piece, (8, LANES)), 16, 1, stride=16, stride_axis=0)

    for k in range(detectors):
        behind = jnp.zeros((8, LANES), jnp.float32)
        older = jnp.zeros((8, LANES), jnp.float32)
        for a in range(blocks):
            now0, now1 = turned(k, a, 0), turned(k, a, 1)
            near = jnp.where(first, now0, now1)
            far = jnp.where(first, now1, behind)
            hankel[k, a, :, 0:LANES] = jnp.concatenate([far, near], axis=0).astype(jnp.bfloat16)
            hankel[k, a, :, LANES:] = jnp.concatenate([older, far], axis=0).astype(jnp.bfloat16)
            behind, older = now0, near

    padded = jnp.concatenate([g_ref[0], jnp.zeros((rows, BLOCK), jnp.float32)], axis=1)
    for p in range(PHASES):
        shift = PHASES - 1 - p
        moved = padded if shift == 0 else pltpu.roll(padded, shift, 1)
        toeplitz[p * rows : (p + 1) * rows, :] = moved.astype(jnp.bfloat16)

    def convolve(groups):
        sides = []
        for k in range(detectors):
            sides.append(
                jnp.concatenate(
                    [
                        hankel[k, depth - 1 - c : depth - 1 - c + groups].reshape(groups * 16, BLOCK)
                        for c in range(depth)
                    ],
                    axis=1,
                )
            )
        return lax.dot_general(
            toeplitz[...],
            jnp.concatenate(sides, axis=0),
            (((1,), (1,)), ((), ())),
            preferred_element_type=jnp.float32,
        )

    rate = rates[step]

    @pl.when(rate == 1)
    def _():
        full[...] += convolve(16)

    @pl.when(rate == 2)
    def _():
        half[...] += convolve(8)

    @pl.when(rate > 2)
    def _():
        small[(rate > 4).astype(jnp.int32)] += convolve(4)

    @pl.when(step == last)
    def _():
        lane = lax.broadcasted_iota(jnp.int32, (rows, LANES), 1)
        for k in range(detectors):
            for tile in range(2):
                q = lane + tile * LANES
                total = [
                    full[p * rows : (p + 1) * rows, (2 * k + tile) * LANES : (2 * k + tile + 1) * LANES]
                    for p in range(PHASES)
                ]
                for level in (1, 2, 3):
                    each, count = 1 << level, PHASES >> level
                    source = (q >> level) + (0 if level == 1 else 64 * k)
                    for c in range(count):
                        value = None
                        for phase in range(each):
                            p = phase * count + c
                            if level == 1:
                                piece = half[p * rows : (p + 1) * rows, k * LANES : (k + 1) * LANES]
                            else:
                                piece = small[level - 2, p * rows : (p + 1) * rows, :]
                            piece = jnp.take_along_axis(piece, source, axis=1)
                            value = piece if value is None else jnp.where((q & (each - 1)) == phase, piece, value)
                        for p in range(c * each, (c + 1) * each):
                            total[p] = total[p] + value
                for p in range(PHASES):
                    spread[k, p, :, tile * LANES : (tile + 1) * LANES] = total[p]
            ending = lane == LANES - 1
            for a in range(1, 4):
                for p in range(PHASES):
                    low = pltpu.roll(spread[k, (a - 1) * PHASES + p, :, 0:LANES], LANES - 1, 1)
                    high = pltpu.roll(spread[k, (a - 1) * PHASES + p, :, LANES:], LANES - 1, 1)
                    spread[k, a * PHASES + p, :, 0:LANES] = jnp.where(ending, high, low)
                    spread[k, a * PHASES + p, :, LANES:] = jnp.where(ending, 0.0, high)
        group = 4
        tiles = [[], []]
        for start in range(0, PHASES, group):

            def direction(number, highest):
                one = antenna[number, 0] * spread[0, pl.ds(start + delays[number, 0], group)]
                two = antenna[number, 1] * spread[1, pl.ds(start + delays[number, 1], group)]
                return jnp.maximum(highest, jnp.abs(one + two))

            highest = lax.fori_loop(
                0, directions, direction, jnp.zeros((group, rows, 2 * LANES), jnp.float32), unroll=2
            )
            for p in range(group):
                full[(start + p) * rows : (start + p + 1) * rows, 0 : 2 * LANES] = highest[p]
        for tile in range(2):
            mixed = interleave(
                [full[p * rows : (p + 1) * rows, tile * LANES : (tile + 1) * LANES] for p in range(PHASES)], lane
            )
            for v in range(PHASES):
                at = 16 * tile + ((v & 7) << 1) + (v >> 3)
                out_ref[:, at * LANES : (at + 1) * LANES] = mixed[v]


def shards(strain, filters, recon_weights, row_spans, slice_rates, delays, antenna):
    slice_index = lax.axis_index("cuts")
    slices = lax.axis_size("cuts")
    detector = lax.axis_index("det")
    detectors = lax.axis_size("det")
    bases, taps = filters.shape[1:]
    share = recon_weights.shape[1] // (slices * detectors)
    window = strain.shape[2] - taps
    blocks = strain.shape[2] // BLOCK
    weights = lax.dynamic_index_in_dim(
        recon_weights[0].reshape(slices, detectors, share, bases), detector, 1, keepdims=False
    )
    spans = lax.dynamic_index_in_dim(row_spans.reshape(slices, detectors, share), detector, 1, keepdims=False)
    composite = jnp.dot(weights.reshape(slices * share, bases), filters[0], preferred_element_type=jnp.float32)
    composite = composite.reshape(slices, share, taps) * (slice_index < spans).astype(jnp.float32)[:, :, None]
    exchange = (lax.broadcasted_iota(jnp.int32, (BLOCK, BLOCK), 0) + lax.broadcasted_iota(jnp.int32, (BLOCK, BLOCK), 1)
                == BLOCK - 1).astype(jnp.bfloat16)
    backward = jnp.dot(strain[0, 0].reshape(blocks, BLOCK), exchange, preferred_element_type=jnp.float32)
    backward = lax.all_gather(backward, ("cuts", "det")).reshape(slices, detectors, blocks, BLOCK)
    received = lax.all_to_all(composite, "cuts", split_axis=0, concat_axis=0, tiled=True)
    depth = taps + BLOCK
    return pl.pallas_call(
        kernel,
        out_shape=jax.ShapeDtypeStruct((share, window), jnp.float32),
        grid_spec=pltpu.PrefetchScalarGridSpec(
            num_scalar_prefetch=3,
            grid=(slices,),
            in_specs=[
                pl.BlockSpec((1, share, taps), lambda i, *_: (i, 0, 0)),
                pl.BlockSpec((1, detectors, blocks, BLOCK), lambda i, *_: (i, 0, 0, 0)),
            ],
            out_specs=pl.BlockSpec((share, window), lambda i, *_: (0, 0)),
            scratch_shapes=[
                pltpu.VMEM((PHASES * share, depth), jnp.bfloat16),
                pltpu.VMEM((detectors, blocks, 16, BLOCK), jnp.bfloat16),
                pltpu.VMEM((PHASES * share, detectors * 256), jnp.float32),
                pltpu.VMEM((PHASES * share, detectors * 128), jnp.float32),
                pltpu.VMEM((2, PHASES * share, detectors * 64), jnp.float32),
                pltpu.VMEM((detectors, 4 * PHASES, share, 256), jnp.float32),
            ],
        ),
        compiler_params=pltpu.CompilerParams(
            vmem_limit_bytes=32 * 1024 * 1024, dimension_semantics=("arbitrary",)
        ),
    )(slice_rates, delays, antenna, received, backward)


def solution(mesh):
    placed = (
        P("cuts", "det", None),
        P(("bank", "cuts"), None, None),
        P(("bank", "cuts"), None, None),
        P("bank"),
        P(),
        P(),
        P(),
    )
    return jax.shard_map(
        shards,
        mesh=mesh,
        in_specs=placed,
        out_specs=P(("bank", "cuts", "det"), None),
        check_vma=False,
    )
```

```python
import jax
import jax.numpy as jnp
from jax import lax
from jax.experimental import pallas as pl
from jax.experimental.pallas import tpu as pltpu
from jax.sharding import PartitionSpec as P

PHASES = 16
LANES = 128
BLOCK = 256


def compose(weights_ref, filters_ref, strain_ref, out_ref):
    step = pl.program_id(0)
    last = pl.num_programs(0) - 1
    targets, share = out_ref.shape[0], weights_ref.shape[1]
    tiles = out_ref.shape[1] // share

    @pl.when(step < last)
    def _():
        rows = jnp.dot(
            weights_ref[...].reshape(targets * share, -1), filters_ref[...], preferred_element_type=jnp.float32
        )
        for tile in range(tiles):
            out_ref[:, tile * share : (tile + 1) * share, :] = rows[:, tile * LANES : (tile + 1) * LANES].reshape(
                targets, share, LANES
            )

    @pl.when(step == last)
    def _():
        flip = (
            lax.broadcasted_iota(jnp.int32, (LANES, LANES), 0) + lax.broadcasted_iota(jnp.int32, (LANES, LANES), 1)
            == LANES - 1
        ).astype(jnp.bfloat16)
        backward = jnp.dot(strain_ref[...], flip, preferred_element_type=jnp.float32)
        for target in range(targets):
            out_ref[target, 0 : backward.shape[0], :] = backward


def interleave(tiles, lane):
    def swap(tiles, bit, lane_bit):
        step = 1 << lane_bit
        upper = (lane & step) != 0
        result = list(tiles)
        for v in range(PHASES):
            if v & (1 << bit):
                continue
            low, high = tiles[v], tiles[v | (1 << bit)]
            result[v] = jnp.where(upper, pltpu.roll(high, step, 1), low)
            result[v | (1 << bit)] = jnp.where(upper, high, pltpu.roll(low, LANES - step, 1))
        return result

    for bit in range(4):
        tiles = swap(tiles, bit, bit)
    for bit in range(3):
        tiles = swap(tiles, bit, bit + 4)
    return tiles


def kernel(rates, spans, delays, antenna, place, g_ref, other_ref, out_ref, toeplitz, hankel, full, half, small, spread, keep):
    step = pl.program_id(0)
    last = pl.num_programs(0) - 1
    rows = out_ref.shape[0]
    tiles = (g_ref.shape[1] - other_ref.shape[1]) // rows
    taps = tiles * LANES
    detectors, blocks = hankel.shape[0], hankel.shape[1]
    depth = taps // BLOCK + 1
    directions = delays.shape[0]

    @pl.when(step == 0)
    def _():
        full[...] = jnp.zeros_like(full)
        half[...] = jnp.zeros_like(half)
        small[...] = jnp.zeros_like(small)
        row = lax.broadcasted_iota(jnp.int32, (rows, LANES), 0)
        span = jnp.zeros((rows, LANES), jnp.int32)
        for r in range(rows):
            span = jnp.where(row == r, spans[place[0] * rows + r], span)
        keep[...] = span

    lane8 = lax.broadcasted_iota(jnp.int32, (8, LANES), 1)
    turn = 16 + 16 * lax.broadcasted_iota(jnp.int32, (8, LANES), 0)
    first = lane8 < turn

    def windows():
        for k, (ref, base) in enumerate(((g_ref, tiles * rows), (other_ref, 0))):

            def turned(a, tile):
                at = base + 2 * a + 1 - tile
                piece = ref[0, at : at + 1, :]
                return pltpu.roll(jnp.broadcast_to(piece, (8, LANES)), 16, 1, stride=16, stride_axis=0)

            behind = jnp.zeros((8, LANES), jnp.float32)
            older = jnp.zeros((8, LANES), jnp.float32)
            for a in range(blocks):
                now0, now1 = turned(a, 0), turned(a, 1)
                near = jnp.where(first, now0, now1)
                far = jnp.where(first, now1, behind)
                hankel[k, a, :, 0:LANES] = jnp.concatenate([far, near], axis=0).astype(jnp.bfloat16)
                hankel[k, a, :, LANES:] = jnp.concatenate([older, far], axis=0).astype(jnp.bfloat16)
                behind, older = now0, near

    def shifted():
        kept = (step < keep[...]).astype(jnp.float32)
        parts = [g_ref[0, t * rows : (t + 1) * rows, :] * kept for t in range(tiles)]
        padded = jnp.concatenate(parts + [jnp.zeros((rows, BLOCK), jnp.float32)], axis=1)
        for p in range(PHASES):
            shift = PHASES - 1 - p
            moved = padded if shift == 0 else pltpu.roll(padded, shift, 1)
            toeplitz[p * rows : (p + 1) * rows, :] = moved.astype(jnp.bfloat16)

    def convolve(groups):
        windows()
        shifted()
        sides = []
        for k in range(detectors):
            sides.append(
                jnp.concatenate(
                    [
                        hankel[k, depth - 1 - c : depth - 1 - c + groups].reshape(groups * 16, BLOCK)
                        for c in range(depth)
                    ],
                    axis=1,
                )
            )
        return lax.dot_general(
            toeplitz[...],
            jnp.concatenate(sides, axis=0),
            (((1,), (1,)), ((), ())),
            preferred_element_type=jnp.float32,
        )

    rate = rates[step]

    @pl.when(rate == 1)
    def _():
        full[...] += convolve(16)

    @pl.when(rate == 2)
    def _():
        half[...] += convolve(8)

    @pl.when(rate > 2)
    def _():
        small[(rate > 4).astype(jnp.int32)] += convolve(4)

    @pl.when(step == last)
    def _():
        lane = lax.broadcasted_iota(jnp.int32, (rows, LANES), 1)
        for k in range(detectors):
            for tile in range(2):
                q = lane + tile * LANES
                total = [
                    full[p * rows : (p + 1) * rows, (2 * k + tile) * LANES : (2 * k + tile + 1) * LANES]
                    for p in range(PHASES)
                ]
                for level in (1, 2, 3):
                    each, count = 1 << level, PHASES >> level
                    source = (q >> level) + (0 if level == 1 else 64 * k)
                    for c in range(count):
                        value = None
                        for phase in range(each):
                            p = phase * count + c
                            if level == 1:
                                piece = half[p * rows : (p + 1) * rows, k * LANES : (k + 1) * LANES]
                            else:
                                piece = small[level - 2, p * rows : (p + 1) * rows, :]
                            piece = jnp.take_along_axis(piece, source, axis=1)
                            value = piece if value is None else jnp.where((q & (each - 1)) == phase, piece, value)
                        for p in range(c * each, (c + 1) * each):
                            total[p] = total[p] + value
                for p in range(PHASES):
                    spread[k, p, :, tile * LANES : (tile + 1) * LANES] = total[p]
            ending = lane == LANES - 1
            for a in range(1, 4):
                for p in range(PHASES):
                    low = pltpu.roll(spread[k, (a - 1) * PHASES + p, :, 0:LANES], LANES - 1, 1)
                    high = pltpu.roll(spread[k, (a - 1) * PHASES + p, :, LANES:], LANES - 1, 1)
                    spread[k, a * PHASES + p, :, 0:LANES] = jnp.where(ending, high, low)
                    spread[k, a * PHASES + p, :, LANES:] = jnp.where(ending, 0.0, high)
        own, other = place[1], 1 - place[1]
        group = 4
        for start in range(0, PHASES, group):

            def direction(number, highest):
                one = antenna[number, own] * spread[0, pl.ds(start + delays[number, own], group)]
                two = antenna[number, other] * spread[1, pl.ds(start + delays[number, other], group)]
                return jnp.maximum(highest, jnp.abs(one + two))

            highest = lax.fori_loop(
                0, directions, direction, jnp.zeros((group, rows, 2 * LANES), jnp.float32), unroll=8
            )
            for p in range(group):
                full[(start + p) * rows : (start + p + 1) * rows, 0 : 2 * LANES] = highest[p]
        for tile in range(2):
            mixed = interleave(
                [full[p * rows : (p + 1) * rows, tile * LANES : (tile + 1) * LANES] for p in range(PHASES)], lane
            )
            for v in range(PHASES):
                at = 16 * tile + ((v & 7) << 1) + (v >> 3)
                out_ref[:, at * LANES : (at + 1) * LANES] = mixed[v]


def shards(strain, filters, recon_weights, row_spans, slice_rates, delays, antenna):
    slice_index = lax.axis_index("cuts")
    slices = lax.axis_size("cuts")
    detector = lax.axis_index("det")
    detectors = lax.axis_size("det")
    bases, taps = filters.shape[1:]
    share = recon_weights.shape[1] // (slices * detectors)
    window = strain.shape[2] - taps
    tiles = strain.shape[2] // LANES
    place = jnp.stack([slice_index * detectors + detector, detector]).astype(jnp.int32)
    steps = 4
    body = taps // steps // LANES * share
    message = pl.pallas_call(
        lambda place, *refs: compose(*refs),
        out_shape=jax.ShapeDtypeStruct((slices, taps // LANES * share + tiles, LANES), jnp.float32),
        grid_spec=pltpu.PrefetchScalarGridSpec(
            num_scalar_prefetch=1,
            grid=(steps + 1,),
            in_specs=[
                pl.BlockSpec((slices, None, share, bases), lambda i, place: (0, place[1], 0, 0)),
                pl.BlockSpec((None, bases, taps // steps), lambda i, place: (0, 0, jnp.minimum(i, steps - 1))),
                pl.BlockSpec((tiles, LANES), lambda i, place: (0, 0)),
            ],
            out_specs=pl.BlockSpec((slices, body, LANES), lambda i, place: (0, i, 0)),
        ),
        compiler_params=pltpu.CompilerParams(
            vmem_limit_bytes=32 * 1024 * 1024, dimension_semantics=("arbitrary",)
        ),
    )(place, recon_weights.reshape(slices, detectors, share, bases), filters, strain.reshape(tiles, LANES))
    received = lax.all_to_all(message, "cuts", split_axis=0, concat_axis=0, tiled=True)
    body = taps // LANES * share
    partner = lax.ppermute(received[:, body:], "det", [(0, 1), (1, 0)])
    depth = taps + BLOCK
    return pl.pallas_call(
        kernel,
        out_shape=jax.ShapeDtypeStruct((share, window), jnp.float32),
        grid_spec=pltpu.PrefetchScalarGridSpec(
            num_scalar_prefetch=5,
            grid=(slices,),
            in_specs=[
                pl.BlockSpec((1, body + tiles, LANES), lambda i, *_: (i, 0, 0)),
                pl.BlockSpec((1, tiles, LANES), lambda i, *_: (i, 0, 0)),
            ],
            out_specs=pl.BlockSpec((share, window), lambda i, *_: (0, 0)),
            scratch_shapes=[
                pltpu.VMEM((PHASES * share, depth), jnp.bfloat16),
                pltpu.VMEM((detectors, tiles // 2, 16, BLOCK), jnp.bfloat16),
                pltpu.VMEM((PHASES * share, detectors * 256), jnp.float32),
                pltpu.VMEM((PHASES * share, detectors * 128), jnp.float32),
                pltpu.VMEM((2, PHASES * share, detectors * 64), jnp.float32),
                pltpu.VMEM((detectors, 4 * PHASES, share, 256), jnp.float32),
                pltpu.VMEM((share, LANES), jnp.int32),
            ],
        ),
        compiler_params=pltpu.CompilerParams(
            vmem_limit_bytes=32 * 1024 * 1024, dimension_semantics=("arbitrary",)
        ),
    )(slice_rates, row_spans, delays, antenna, place, received, partner)


def solution(mesh):
    placed = (
        P("cuts", "det", None),
        P(("bank", "cuts"), None, None),
        P(("bank", "cuts"), None, None),
        P("bank"),
        P(),
        P(),
        P(),
    )
    return jax.shard_map(
        shards,
        mesh=mesh,
        in_specs=placed,
        out_specs=P(("bank", "cuts", "det"), None),
        check_vma=False,
    )
```

```python
import jax
import jax.numpy as jnp
from jax import lax
from jax.experimental import pallas as pl
from jax.experimental.pallas import tpu as pltpu
from jax.sharding import PartitionSpec as P

PHASES = 16
LANES = 128
BLOCK = 256
SLOTS = 4


def compose(place, weights_ref, filters_ref, strain_ref, out_ref, weights, filters, got, arrived):
    chunks, _, width = filters.shape
    targets, share, bases = weights.shape
    here = pltpu.make_async_copy(weights_ref.at[:, place[1]], weights, got)
    here.start()
    parts = [
        pltpu.make_async_copy(
            filters_ref.at[0, :, chunk * width : (chunk + 1) * width], filters.at[chunk], arrived.at[chunk]
        )
        for chunk in range(chunks)
    ]
    for part in parts:
        part.start()
    end = out_ref.shape[1]
    count = strain_ref.shape[0]
    flip = (
        lax.broadcasted_iota(jnp.int32, (LANES, LANES), 0) + lax.broadcasted_iota(jnp.int32, (LANES, LANES), 1)
        == LANES - 1
    ).astype(jnp.bfloat16)
    backward = jnp.dot(strain_ref[...], flip, preferred_element_type=jnp.float32)
    for target in range(targets):
        out_ref[target, end - count : end, :] = backward
    here.wait()
    for chunk, part in enumerate(parts):
        part.wait()
        rows = jnp.dot(
            weights[...].reshape(targets * share, bases), filters[chunk], preferred_element_type=jnp.float32
        )
        for tile in range(width // LANES):
            at = chunk * width // LANES + tile
            out_ref[:, at * share : (at + 1) * share, :] = rows[:, tile * LANES : (tile + 1) * LANES].reshape(
                targets, share, LANES
            )


def interleave(tiles, lane):
    def swap(tiles, bit, lane_bit):
        step = 1 << lane_bit
        upper = (lane & step) != 0
        result = list(tiles)
        for v in range(PHASES):
            if v & (1 << bit):
                continue
            low, high = tiles[v], tiles[v | (1 << bit)]
            result[v] = jnp.where(upper, pltpu.roll(high, step, 1), low)
            result[v | (1 << bit)] = jnp.where(upper, high, pltpu.roll(low, LANES - step, 1))
        return result

    for bit in range(4):
        tiles = swap(tiles, bit, bit)
    for bit in range(3):
        tiles = swap(tiles, bit, bit + 4)
    return tiles


def kernel(rates, spans, delays, antenna, place, g_ref, other_ref, out_ref, toeplitz, hankel, full, half, small, spread):
    slices = g_ref.shape[0]
    detectors, blocks = hankel.shape[1], hankel.shape[2]
    rows = out_ref.shape[0]
    tiles = (g_ref.shape[1] - other_ref.shape[1]) // rows
    taps = tiles * LANES
    depth = taps // BLOCK + 1
    directions = delays.shape[0]

    full[...] = jnp.zeros_like(full)
    half[...] = jnp.zeros_like(half)
    small[...] = jnp.zeros_like(small)
    row = lax.broadcasted_iota(jnp.int32, (rows, LANES), 0)
    keep = jnp.zeros((rows, LANES), jnp.int32)
    for r in range(rows):
        keep = jnp.where(row == r, spans[place[0] * rows + r], keep)
    lane8 = lax.broadcasted_iota(jnp.int32, (8, LANES), 1)
    turn = 16 + 16 * lax.broadcasted_iota(jnp.int32, (8, LANES), 0)
    first = lane8 < turn

    def windows(number, slot, groups):
        for k, (ref, base) in enumerate(((g_ref, tiles * rows), (other_ref, 0))):

            def turned(a, tile):
                at = base + 2 * a + 1 - tile
                piece = ref[number, at : at + 1, :]
                return pltpu.roll(jnp.broadcast_to(piece, (8, LANES)), 16, 1, stride=16, stride_axis=0)

            behind = jnp.zeros((8, LANES), jnp.float32)
            older = jnp.zeros((8, LANES), jnp.float32)
            for a in range(depth - 1 + groups):
                now0, now1 = turned(a, 0), turned(a, 1)
                near = jnp.where(first, now0, now1)
                far = jnp.where(first, now1, behind)
                hankel[slot, k, a, :, 0:LANES] = jnp.concatenate([far, near], axis=0).astype(jnp.bfloat16)
                hankel[slot, k, a, :, LANES:] = jnp.concatenate([older, far], axis=0).astype(jnp.bfloat16)
                behind, older = now0, near

    def shifted(number, slot):
        kept = (number < keep).astype(jnp.float32)
        parts = [g_ref[number, t * rows : (t + 1) * rows, :] * kept for t in range(tiles)]
        padded = jnp.concatenate(parts + [jnp.zeros((rows, BLOCK), jnp.float32)], axis=1).astype(jnp.bfloat16)
        for p in range(PHASES):
            shift = PHASES - 1 - p
            moved = padded if shift == 0 else pltpu.roll(padded, shift, 1)
            toeplitz[p * rows : (p + 1) * rows, slot * depth * BLOCK : (slot + 1) * depth * BLOCK] = moved

    def convolve(number, slots, groups):
        for slot in slots:
            shifted(number + slot, slot)
            windows(number + slot, slot, groups)
        sides = []
        for k in range(detectors):
            sides.append(
                jnp.concatenate(
                    [
                        hankel[slot, k, depth - 1 - c : depth - 1 - c + groups].reshape(groups * 16, BLOCK)
                        for slot in slots
                        for c in range(depth)
                    ],
                    axis=1,
                )
            )
        return lax.dot_general(
            toeplitz[:, slots[0] * depth * BLOCK : (slots[-1] + 1) * depth * BLOCK],
            jnp.concatenate(sides, axis=0),
            (((1,), (1,)), ((), ())),
            preferred_element_type=jnp.float32,
        )

    start = 0
    for total, groups, rate in ((full, 16, 1), (half, 8, 2), (small.at[0], 4, 4), (small.at[1], 4, 8)):
        count = lax.fori_loop(0, slices, lambda i, n, rate=rate: n + (rates[i] == rate).astype(jnp.int32), 0)
        done = start
        size = SLOTS
        while size:
            left = start + count - done

            def several(index, carry, done=done, size=size, total=total, groups=groups):
                total[...] += convolve(done + index * size, tuple(range(size)), groups)
                return carry

            times = left // size
            lax.fori_loop(0, times, several, 0)
            done = done + times * size
            size //= 2
        start = start + count

    lane = lax.broadcasted_iota(jnp.int32, (rows, LANES), 1)
    for k in range(detectors):
        for tile in range(2):
            q = lane + tile * LANES
            total = [
                full[p * rows : (p + 1) * rows, (2 * k + tile) * LANES : (2 * k + tile + 1) * LANES]
                for p in range(PHASES)
            ]
            for level in (1, 2, 3):
                each, count = 1 << level, PHASES >> level
                source = (q >> level) + (0 if level == 1 else 64 * k)
                for c in range(count):
                    value = None
                    for phase in range(each):
                        p = phase * count + c
                        if level == 1:
                            piece = half[p * rows : (p + 1) * rows, k * LANES : (k + 1) * LANES]
                        else:
                            piece = small[level - 2, p * rows : (p + 1) * rows, :]
                        piece = jnp.take_along_axis(piece, source, axis=1)
                        value = piece if value is None else jnp.where((q & (each - 1)) == phase, piece, value)
                    for p in range(c * each, (c + 1) * each):
                        total[p] = total[p] + value
            for p in range(PHASES):
                spread[k, p, :, tile * LANES : (tile + 1) * LANES] = total[p]
        ending = lane == LANES - 1
        for a in range(1, 4):
            for p in range(PHASES):
                low = pltpu.roll(spread[k, (a - 1) * PHASES + p, :, 0:LANES], LANES - 1, 1)
                high = pltpu.roll(spread[k, (a - 1) * PHASES + p, :, LANES:], LANES - 1, 1)
                spread[k, a * PHASES + p, :, 0:LANES] = jnp.where(ending, high, low)
                spread[k, a * PHASES + p, :, LANES:] = jnp.where(ending, 0.0, high)
    own, other = place[1], 1 - place[1]
    group = 4
    for start in range(0, PHASES, group):

        def direction(number, highest):
            one = antenna[number, own] * spread[0, pl.ds(start + delays[number, own], group)]
            two = antenna[number, other] * spread[1, pl.ds(start + delays[number, other], group)]
            return jnp.maximum(highest, jnp.abs(one + two))

        highest = lax.fori_loop(
            0, directions, direction, jnp.zeros((group, rows, 2 * LANES), jnp.float32), unroll=8
        )
        for p in range(group):
            full[(start + p) * rows : (start + p + 1) * rows, 0 : 2 * LANES] = highest[p]
    for tile in range(2):
        mixed = interleave(
            [full[p * rows : (p + 1) * rows, tile * LANES : (tile + 1) * LANES] for p in range(PHASES)], lane
        )
        for v in range(PHASES):
            at = 16 * tile + ((v & 7) << 1) + (v >> 3)
            out_ref[:, at * LANES : (at + 1) * LANES] = mixed[v]


def shards(strain, filters, recon_weights, row_spans, slice_rates, delays, antenna):
    slice_index = lax.axis_index("cuts")
    slices = lax.axis_size("cuts")
    detector = lax.axis_index("det")
    detectors = lax.axis_size("det")
    bases, taps = filters.shape[1:]
    share = recon_weights.shape[1] // (slices * detectors)
    window = strain.shape[2] - taps
    tiles = strain.shape[2] // LANES
    place = jnp.stack([slice_index * detectors + detector, detector]).astype(jnp.int32)
    chunks = 4
    message = pl.pallas_call(
        compose,
        out_shape=jax.ShapeDtypeStruct((slices, taps // LANES * share + tiles, LANES), jnp.float32),
        in_specs=[
            pl.BlockSpec(memory_space=pltpu.SMEM),
            pl.BlockSpec(memory_space=pltpu.HBM),
            pl.BlockSpec(memory_space=pltpu.HBM),
            pl.BlockSpec(memory_space=pltpu.VMEM),
        ],
        out_specs=pl.BlockSpec(memory_space=pltpu.VMEM),
        scratch_shapes=[
            pltpu.VMEM((slices, share, bases), jnp.bfloat16),
            pltpu.VMEM((chunks, bases, taps // chunks), jnp.bfloat16),
            pltpu.SemaphoreType.DMA,
            pltpu.SemaphoreType.DMA((chunks,)),
        ],
        compiler_params=pltpu.CompilerParams(vmem_limit_bytes=32 * 1024 * 1024),
    )(place, recon_weights.reshape(slices, detectors, share, bases), filters, strain.reshape(tiles, LANES))
    received = lax.all_to_all(message, "cuts", split_axis=0, concat_axis=0, tiled=True)
    body = taps // LANES * share
    partner = lax.ppermute(received[:, body:], "det", [(0, 1), (1, 0)])
    depth = taps + BLOCK
    return pl.pallas_call(
        kernel,
        out_shape=jax.ShapeDtypeStruct((share, window), jnp.float32),
        in_specs=[pl.BlockSpec(memory_space=pltpu.SMEM)] * 5 + [pl.BlockSpec(memory_space=pltpu.VMEM)] * 2,
        out_specs=pl.BlockSpec(memory_space=pltpu.VMEM),
        scratch_shapes=[
            pltpu.VMEM((PHASES * share, SLOTS * depth), jnp.bfloat16),
            pltpu.VMEM((SLOTS, detectors, tiles // 2, 16, BLOCK), jnp.bfloat16),
            pltpu.VMEM((PHASES * share, detectors * 256), jnp.float32),
            pltpu.VMEM((PHASES * share, detectors * 128), jnp.float32),
            pltpu.VMEM((2, PHASES * share, detectors * 64), jnp.float32),
            pltpu.VMEM((detectors, 4 * PHASES, share, 256), jnp.float32),
        ],
        compiler_params=pltpu.CompilerParams(vmem_limit_bytes=32 * 1024 * 1024),
    )(slice_rates, row_spans, delays, antenna, place, received, partner)


def solution(mesh):
    placed = (
        P("cuts", "det", None),
        P(("bank", "cuts"), None, None),
        P(("bank", "cuts"), None, None),
        P("bank"),
        P(),
        P(),
        P(),
    )
    return jax.shard_map(
        shards,
        mesh=mesh,
        in_specs=placed,
        out_specs=P(("bank", "cuts", "det"), None),
        check_vma=False,
    )
```

```python
import jax
import jax.numpy as jnp
from jax import lax
from jax.experimental import pallas as pl
from jax.experimental.pallas import tpu as pltpu
from jax.sharding import PartitionSpec as P

PHASES = 16
LANES = 128
BLOCK = 256
SLOTS = 4


def compose(place, weights_ref, filters_ref, strain_ref, out_ref):
    targets, _, share, bases = weights_ref.shape
    taps, width = filters_ref.shape[2], 4 * LANES
    end, count = out_ref.shape[1], strain_ref.shape[0]
    flip = (
        lax.broadcasted_iota(jnp.int32, (LANES, LANES), 0) + lax.broadcasted_iota(jnp.int32, (LANES, LANES), 1)
        == LANES - 1
    ).astype(jnp.bfloat16)
    backward = jnp.dot(strain_ref[...], flip, preferred_element_type=jnp.float32)
    for target in range(targets):
        out_ref[target, end - count : end, :] = backward
    weights = weights_ref[:, place[1]].reshape(targets * share, bases)
    for chunk in range(taps // width):
        rows = jnp.dot(
            weights, filters_ref[0, :, chunk * width : (chunk + 1) * width], preferred_element_type=jnp.float32
        )
        for tile in range(width // LANES):
            at = chunk * width // LANES + tile
            out_ref[:, at * share : (at + 1) * share, :] = rows[:, tile * LANES : (tile + 1) * LANES].reshape(
                targets, share, LANES
            )


def interleave(tiles, lane):
    def swap(tiles, bit, lane_bit):
        step = 1 << lane_bit
        upper = (lane & step) != 0
        result = list(tiles)
        for v in range(PHASES):
            if v & (1 << bit):
                continue
            low, high = tiles[v], tiles[v | (1 << bit)]
            result[v] = jnp.where(upper, pltpu.roll(high, step, 1), low)
            result[v | (1 << bit)] = jnp.where(upper, high, pltpu.roll(low, LANES - step, 1))
        return result

    for bit in range(4):
        tiles = swap(tiles, bit, bit)
    for bit in range(3):
        tiles = swap(tiles, bit, bit + 4)
    return tiles


def kernel(rates, spans, delays, antenna, place, g_ref, other_ref, out_ref, toeplitz, hankel, full, half, small, spread):
    slices = g_ref.shape[0]
    detectors, blocks = hankel.shape[1], hankel.shape[2]
    rows = out_ref.shape[0]
    tiles = (g_ref.shape[1] - other_ref.shape[1]) // rows
    taps = tiles * LANES
    depth = taps // BLOCK + 1
    directions = delays.shape[0]

    full[...] = jnp.zeros_like(full)
    half[...] = jnp.zeros_like(half)
    small[...] = jnp.zeros_like(small)
    row = lax.broadcasted_iota(jnp.int32, (rows, LANES), 0)
    keep = jnp.zeros((rows, LANES), jnp.int32)
    for r in range(rows):
        keep = jnp.where(row == r, spans[place[0] * rows + r], keep)
    lane8 = lax.broadcasted_iota(jnp.int32, (8, LANES), 1)
    turn = 16 + 16 * lax.broadcasted_iota(jnp.int32, (8, LANES), 0)
    first = lane8 < turn

    def windows(number, slot, groups):
        for k, (ref, base) in enumerate(((g_ref, tiles * rows), (other_ref, 0))):

            def turned(a, tile):
                at = base + 2 * a + 1 - tile
                piece = ref[number, at : at + 1, :]
                return pltpu.roll(jnp.broadcast_to(piece, (8, LANES)), 16, 1, stride=16, stride_axis=0)

            behind = jnp.zeros((8, LANES), jnp.float32)
            older = jnp.zeros((8, LANES), jnp.float32)
            for a in range(depth - 1 + groups):
                now0, now1 = turned(a, 0), turned(a, 1)
                near = jnp.where(first, now0, now1)
                far = jnp.where(first, now1, behind)
                hankel[slot, k, a, :, 0:LANES] = jnp.concatenate([far, near], axis=0).astype(jnp.bfloat16)
                hankel[slot, k, a, :, LANES:] = jnp.concatenate([older, far], axis=0).astype(jnp.bfloat16)
                behind, older = now0, near

    def shifted(number, slot):
        kept = (number < keep).astype(jnp.float32)
        parts = [g_ref[number, t * rows : (t + 1) * rows, :] * kept for t in range(tiles)]
        padded = jnp.concatenate(parts + [jnp.zeros((rows, BLOCK), jnp.float32)], axis=1).astype(jnp.bfloat16)
        for p in range(PHASES):
            shift = PHASES - 1 - p
            moved = padded if shift == 0 else pltpu.roll(padded, shift, 1)
            toeplitz[p * rows : (p + 1) * rows, slot * depth * BLOCK : (slot + 1) * depth * BLOCK] = moved

    def convolve(number, slots, groups):
        for slot in slots:
            shifted(number + slot, slot)
            windows(number + slot, slot, groups)
        sides = []
        for k in range(detectors):
            sides.append(
                jnp.concatenate(
                    [
                        hankel[slot, k, depth - 1 - c : depth - 1 - c + groups].reshape(groups * 16, BLOCK)
                        for slot in slots
                        for c in range(depth)
                    ],
                    axis=1,
                )
            )
        return lax.dot_general(
            toeplitz[:, slots[0] * depth * BLOCK : (slots[-1] + 1) * depth * BLOCK],
            jnp.concatenate(sides, axis=0),
            (((1,), (1,)), ((), ())),
            preferred_element_type=jnp.float32,
        )

    start = 0
    for total, groups, rate in ((full, 16, 1), (half, 8, 2), (small.at[0], 4, 4), (small.at[1], 4, 8)):
        count = lax.fori_loop(0, slices, lambda i, n, rate=rate: n + (rates[i] == rate).astype(jnp.int32), 0)
        done = start
        size = SLOTS
        while size:
            left = start + count - done

            def several(index, carry, done=done, size=size, total=total, groups=groups):
                total[...] += convolve(done + index * size, tuple(range(size)), groups)
                return carry

            times = left // size
            lax.fori_loop(0, times, several, 0)
            done = done + times * size
            size //= 2
        start = start + count

    lane = lax.broadcasted_iota(jnp.int32, (rows, LANES), 1)
    for k in range(detectors):
        for tile in range(2):
            q = lane + tile * LANES
            total = [
                full[p * rows : (p + 1) * rows, (2 * k + tile) * LANES : (2 * k + tile + 1) * LANES]
                for p in range(PHASES)
            ]
            for level in (1, 2, 3):
                each, count = 1 << level, PHASES >> level
                source = (q >> level) + (0 if level == 1 else 64 * k)
                for c in range(count):
                    value = None
                    for phase in range(each):
                        p = phase * count + c
                        if level == 1:
                            piece = half[p * rows : (p + 1) * rows, k * LANES : (k + 1) * LANES]
                        else:
                            piece = small[level - 2, p * rows : (p + 1) * rows, :]
                        piece = jnp.take_along_axis(piece, source, axis=1)
                        value = piece if value is None else jnp.where((q & (each - 1)) == phase, piece, value)
                    for p in range(c * each, (c + 1) * each):
                        total[p] = total[p] + value
            for p in range(PHASES):
                spread[k, p, :, tile * LANES : (tile + 1) * LANES] = total[p]
        ending = lane == LANES - 1
        for a in range(1, 4):
            for p in range(PHASES):
                low = pltpu.roll(spread[k, (a - 1) * PHASES + p, :, 0:LANES], LANES - 1, 1)
                high = pltpu.roll(spread[k, (a - 1) * PHASES + p, :, LANES:], LANES - 1, 1)
                spread[k, a * PHASES + p, :, 0:LANES] = jnp.where(ending, high, low)
                spread[k, a * PHASES + p, :, LANES:] = jnp.where(ending, 0.0, high)
    own, other = place[1], 1 - place[1]
    group = 4
    for start in range(0, PHASES, group):

        def direction(number, highest):
            one = antenna[number, own] * spread[0, pl.ds(start + delays[number, own], group)]
            two = antenna[number, other] * spread[1, pl.ds(start + delays[number, other], group)]
            return jnp.maximum(highest, jnp.abs(one + two))

        highest = lax.fori_loop(
            0, directions, direction, jnp.zeros((group, rows, 2 * LANES), jnp.float32), unroll=32
        )
        for p in range(group):
            full[(start + p) * rows : (start + p + 1) * rows, 0 : 2 * LANES] = highest[p]
    for tile in range(2):
        mixed = interleave(
            [full[p * rows : (p + 1) * rows, tile * LANES : (tile + 1) * LANES] for p in range(PHASES)], lane
        )
        for v in range(PHASES):
            at = 16 * tile + ((v & 7) << 1) + (v >> 3)
            out_ref[:, at * LANES : (at + 1) * LANES] = mixed[v]


def shards(strain, filters, recon_weights, row_spans, slice_rates, delays, antenna):
    slice_index = lax.axis_index("cuts")
    slices = lax.axis_size("cuts")
    detector = lax.axis_index("det")
    detectors = lax.axis_size("det")
    bases, taps = filters.shape[1:]
    share = recon_weights.shape[1] // (slices * detectors)
    window = strain.shape[2] - taps
    tiles = strain.shape[2] // LANES
    place = jnp.stack([slice_index * detectors + detector, detector]).astype(jnp.int32)
    message = pl.pallas_call(
        compose,
        out_shape=jax.ShapeDtypeStruct((slices, taps // LANES * share + tiles, LANES), jnp.float32),
        in_specs=[pl.BlockSpec(memory_space=pltpu.SMEM)] + [pl.BlockSpec(memory_space=pltpu.VMEM)] * 3,
        out_specs=pl.BlockSpec(memory_space=pltpu.VMEM),
        compiler_params=pltpu.CompilerParams(vmem_limit_bytes=32 * 1024 * 1024),
    )(place, recon_weights.reshape(slices, detectors, share, bases), filters, strain.reshape(tiles, LANES))
    received = lax.all_to_all(message, "cuts", split_axis=0, concat_axis=0, tiled=True)
    body = taps // LANES * share
    partner = lax.ppermute(received[:, body:], "det", [(0, 1), (1, 0)])
    depth = taps + BLOCK
    return pl.pallas_call(
        kernel,
        out_shape=jax.ShapeDtypeStruct((share, window), jnp.float32),
        in_specs=[pl.BlockSpec(memory_space=pltpu.SMEM)] * 5 + [pl.BlockSpec(memory_space=pltpu.VMEM)] * 2,
        out_specs=pl.BlockSpec(memory_space=pltpu.VMEM),
        scratch_shapes=[
            pltpu.VMEM((PHASES * share, SLOTS * depth), jnp.bfloat16),
            pltpu.VMEM((SLOTS, detectors, tiles // 2, 16, BLOCK), jnp.bfloat16),
            pltpu.VMEM((PHASES * share, detectors * 256), jnp.float32),
            pltpu.VMEM((PHASES * share, detectors * 128), jnp.float32),
            pltpu.VMEM((2, PHASES * share, detectors * 64), jnp.float32),
            pltpu.VMEM((detectors, 4 * PHASES, share, 256), jnp.float32),
        ],
        compiler_params=pltpu.CompilerParams(vmem_limit_bytes=32 * 1024 * 1024),
    )(slice_rates, row_spans, delays, antenna, place, received, partner)


def solution(mesh):
    placed = (
        P("cuts", "det", None),
        P(("bank", "cuts"), None, None),
        P(("bank", "cuts"), None, None),
        P("bank"),
        P(),
        P(),
        P(),
    )
    return jax.shard_map(
        shards,
        mesh=mesh,
        in_specs=placed,
        out_specs=P(("bank", "cuts", "det"), None),
        check_vma=False,
    )
```
